128 devices in a mesh: tm: 8 (over x, core), space: 16 (over z, y).
Axes of the slice: x: 4, y: 4, z: 4, core: 2. Of those that a mesh axis runs over, the one named last changes fastest.
Arguments:
- initial_voltage: float32 [4096, 128], P('space'), may hold values from -2 to 2
- initial_recovery: float32 [4096, 128], P('space'), may hold values from -0.5 to 1
- block_class: int32 [512], P('space'), may hold values from 0 to 3
- block_active: int32 [512], P('space'), may hold values 0 or 1
Outputs:
- points: float32 [16, 2, 4096, 128], P('tm', None, 'space')
The draws below stay inside these ranges and needn't reach their ends.
Inputs may be any that keep to these rules, and one draw needn't show every extreme that they name: `block_active`: 1 marks tissue.
All inputs are finite; a program needn't handle non-finite values. No bound on the sum of `block_active` on one device may be relied on, other than what follows from the above.
Results may differ from the reference program's by a relative error of at most 0.00002.
Values sent between devices are 32-bit elements; how exact they have to be, the bound alone decides.
A program may use at most 64 MiB of HBM per device.

```python
import jax
import jax.numpy as jnp

W = 128
BR = 8
NCLASS = 4
CF = 8
ITERS = 2
NY = 4096
NB = 512
NC = 16


def touch_ends(values, own_key, smallest, largest):
    index_at = [jax.random.randint(jax.random.fold_in(own_key, axis), (), 0, length) for axis, length in enumerate(values.shape)]
    widest = values.shape.index(max(values.shape))
    beside = index_at[:widest] + [(index_at[widest] + 1) % values.shape[widest]] + index_at[widest + 1:]
    return values.at[tuple(index_at)].set(smallest).at[tuple(beside)].set(largest)


def block_scale(own_key, shape, pieces, low, high):
    level, own = 1.0, jax.random.fold_in(own_key, 6)
    for dim, parts in pieces:
        steps = jnp.exp(jax.random.uniform(jax.random.fold_in(own, dim), (parts,), jnp.float32, low / len(pieces), high / len(pieces)))
        level = level * jnp.repeat(steps, shape[dim] // parts).reshape([-1 if axis == dim else 1 for axis in range(len(shape))])
    return level


def setup_inputs(seed: int = 0) -> dict:
    seeds = jax.random.split(jax.random.key(seed), 5)
    initial_voltage = jnp.clip(jax.random.uniform(seeds[0], (NY, W), jnp.float32, -2.0, 2.0) * block_scale(seeds[0], (NY, W), ((0, 16),), -0.4, 0.0), -2.0, 2.0)
    initial_recovery = jnp.clip(-0.5 + 1.5 * jax.random.uniform(seeds[1], (NY, W), jnp.float32) ** block_scale(seeds[1], (NY, W), ((0, 16),), -0.2, 0.2), -0.5, 1.0)
    block_class = touch_ends(jax.random.randint(seeds[2], (NB,), 0, NCLASS), jax.random.fold_in(seeds[2], 1), 0, NCLASS - 1).astype(jnp.int32)
    block_active = touch_ends((jax.random.randint(seeds[3], (NB,), 0, 4) < 3).astype(jnp.int32), jax.random.fold_in(seeds[3], 1), 0, 1)
    return {"initial_voltage": initial_voltage, "initial_recovery": initial_recovery, "block_class": block_class, "block_active": block_active}


row_gains = (0.2, 0.35, 0.5, 0.6)
column_gains = (0.6, 0.5, 0.35, 0.2)
rate_gains = (0.06, 0.08, 0.1, 0.13)
fine_length = 0.05


def lookup(classes, table):
    onehot = (classes[:, None] == jnp.arange(NCLASS, dtype=jnp.int32)[None, :]).astype(jnp.float32)
    return jnp.sum(onehot * jnp.array(table, dtype=jnp.float32)[None, :], axis=1)


def advance(voltage_padded, recovery, between, column_coupling, recovery_rate, active, length):
    voltage = voltage_padded[:, 1:-1]
    from_below = between[None, 1:, None] * (voltage_padded[:, 2:] - voltage)
    from_above = between[None, :-1, None] * (voltage_padded[:, :-2] - voltage)
    from_right = jnp.concatenate([voltage[..., 1:], voltage[..., -1:]], axis=-1)
    from_left = jnp.concatenate([voltage[..., :1], voltage[..., :-1]], axis=-1)
    diffusion = from_below + from_above + column_coupling[None, :, None] * (from_right + from_left - 2.0 * voltage)
    reaction = active[None, :, None] * (voltage - voltage ** 3 / 3.0 - recovery)
    new_voltage = voltage + length * (diffusion + reaction)
    new_recovery = recovery + length * recovery_rate[None, :, None] * (voltage + 0.7 - 0.8 * recovery)
    return jnp.stack([new_voltage, new_recovery], axis=1)


def reference(initial_voltage, initial_recovery, block_class, block_active):
    classes = jnp.repeat(block_class, BR)
    active = jnp.repeat(block_active, BR).astype(jnp.float32)
    row_coupling = lookup(classes, row_gains)
    column_coupling = lookup(classes, column_gains) * active
    recovery_rate = lookup(classes, rate_gains) * active
    coupling_pad = jnp.pad(row_coupling, 1)
    active_pad = jnp.pad(active, 1)
    between = 0.5 * (coupling_pad[:-1] + coupling_pad[1:]) * active_pad[:-1] * active_pad[1:]

    def advance_state(state, length):
        padded = jnp.pad(state[:, 0], ((0, 0), (1, 1), (0, 0)))
        return advance(padded, state[:, 1], between, column_coupling, recovery_rate, active, length)

    def propagate(state):
        for repeat_index in range(CF):
            state = advance_state(state, fine_length)
        return state

    start_state = jnp.stack([initial_voltage, initial_recovery])[None]
    points = jnp.broadcast_to(start_state, (NC, 2, NY, W))
    for iteration in range(ITERS):
        before = jnp.concatenate([start_state, points[:-1]], axis=0)
        points = propagate(before)
        before = jnp.concatenate([start_state, points[:-1]], axis=0)
        defect = propagate(before) - advance_state(before, fine_length * CF)
        carried = start_state
        results = []
        for position in range(NC):
            carried = advance_state(carried, fine_length * CF) + defect[position:position + 1]
            results.append(carried)
        points = jnp.concatenate(results, axis=0)
    return points
```

```python
import functools
import math

import jax
import jax.numpy as jnp
from jax import lax
from jax.experimental import pallas as pl
from jax.experimental.pallas import tpu as pltpu
from jax.sharding import PartitionSpec as P

MESH = pl.DeviceIdType.MESH

W = 128
BR = 8
ROWS = 256
HALF = 128
GHOST = 48
WIN = HALF + 2 * GHOST
NBLK = WIN // BR
PAD = 8
LOCAL = HALF + GHOST

row_gains = (0.2, 0.35, 0.5, 0.6)
column_gains = (0.6, 0.5, 0.35, 0.2)
rate_gains = (0.06, 0.08, 0.1, 0.13)
HF = 0.05
HG = 0.05 * 8
SF = math.sqrt(3.0 / HF)
SG = math.sqrt(3.0 / HG)
CX = SF / SG
CY = (SF / HF) / (SG / HG)


def pick(classes, table):
    out = jnp.full_like(classes, table[3])
    for i in (2, 1, 0):
        out = jnp.where(classes == float(i), table[i], out)
    return out


def span(g):
    return (GHOST - g) // 8 * 8, -(-(GHOST + HALF + g) // 8) * 8


def update(x, xu, xd, y, co):
    a0, bu, bd, cl, cr, h1, h2, h3 = co
    near = bu * xu + bd * xd
    side = cl * pltpu.roll(x, 1, 1) + cr * pltpu.roll(x, W - 1, 1)
    return (x * (a0 - x * x) - y + near) + side, h2 * y + (h1 * x + h3)


def step(src, dst, rows, co, extra=None):
    lo, hi = rows[0] + PAD, rows[1] + PAD
    sx, sy = src
    x = sx[lo:hi]
    nx, ny = update(x, sx[lo - 1 : hi - 1], sx[lo + 1 : hi + 1], sy[lo:hi], [co[q, rows[0] : rows[1]] for q in range(8)])
    if extra is not None:
        nx, ny = nx + extra[0][lo:hi], ny + extra[1][lo:hi]
    dst[0][lo:hi] = nx
    dst[1][lo:hi] = ny


def steps_of_lines(src, dst, lines, rows, co):
    for r in range(rows[0], rows[1], 8):
        c = [co[q, r : r + 8] for q in range(8)]
        lo = r + PAD
        for i in range(lines):
            sx, sy = src[0].at[i], src[1].at[i]
            nx, ny = update(sx[lo : lo + 8], sx[lo - 1 : lo + 7], sx[lo + 1 : lo + 9], sy[lo : lo + 8], c)
            dst[0][i, lo : lo + 8] = nx
            dst[1][i, lo : lo + 8] = ny


def kernel(
    u_ref, v_ref, cls_ref, act_ref, out_ref,
    uw, vw, ocls, oact, ncls, nact, tab, mask, cf, cg, fx, fy, px, py, dx, dy, lx, ly, ex, ey, rx, ry, send,
    lsem, ssem, rsem, xs, xr,
):
    t, s = lax.axis_index("tm"), lax.axis_index("space")
    chip, core = lax.div(t, 2), lax.rem(t, 2)
    to = {"space": lax.rem(s + 17 - 2 * core, 16)}
    fro = {"space": lax.rem(s + 15 + 2 * core, 16)}
    mate = {"tm": t + 1 - 2 * core}

    barrier = pltpu.get_barrier_semaphore()
    for peer in (to, fro, mate):
        pl.semaphore_signal(barrier, inc=1, device_id=peer, device_id_type=MESH)

    here = pl.multiple_of(80 * core, 8)
    there = pl.multiple_of(GHOST * (1 - core), 8)
    local = [
        pltpu.make_async_copy(u_ref.at[pl.ds(here, LOCAL)], uw.at[pl.ds(there, LOCAL)], lsem.at[0]),
        pltpu.make_async_copy(v_ref.at[pl.ds(here, LOCAL)], vw.at[pl.ds(there, LOCAL)], lsem.at[1]),
        pltpu.make_async_copy(cls_ref, ocls, lsem.at[2]),
        pltpu.make_async_copy(act_ref, oact, lsem.at[3]),
    ]
    for c in local:
        c.start()
    for buf in (fx, fy):
        for k in range(2):
            buf[k, :PAD] = jnp.zeros((PAD, W), jnp.float32)
            buf[k, PAD + WIN :] = jnp.zeros((PAD, W), jnp.float32)

    pl.semaphore_wait(barrier, 3)
    edge = pl.multiple_of((ROWS - GHOST) * (1 - core), 8)
    land = pl.multiple_of(LOCAL * core, 8)
    remote = []
    for i, (a, b) in enumerate(
        [
            (cls_ref, ncls),
            (act_ref, nact),
            (u_ref.at[pl.ds(edge, GHOST)], uw.at[pl.ds(land, GHOST)]),
            (v_ref.at[pl.ds(edge, GHOST)], vw.at[pl.ds(land, GHOST)]),
        ]
    ):
        c = pltpu.make_async_remote_copy(
            src_ref=a, dst_ref=b, send_sem=ssem.at[i], recv_sem=rsem.at[i], device_id=to, device_id_type=MESH
        )
        c.start()
        remote.append(c)
    for c in local:
        c.wait()
    for c in remote:
        c.wait()

    wi = lax.broadcasted_iota(jnp.int32, (32, 32), 0) + (16 * core - GHOST // BR)
    lane = lax.broadcasted_iota(jnp.int32, (32, 32), 1)
    own = (wi >= 0) & (wi < 32)
    hot = lane == jnp.where(wi < 0, wi + 32, jnp.where(wi >= 32, wi - 32, wi))
    gi = wi + 32 * s
    inside = (gi >= 0) & (gi < 512)
    cls = jnp.where(own, jnp.broadcast_to(ocls[...], (32, 32)), jnp.broadcast_to(ncls[...], (32, 32)))
    act = jnp.where(own, jnp.broadcast_to(oact[...], (32, 32)), jnp.broadcast_to(nact[...], (32, 32)))
    cls = jnp.where(hot, cls.astype(jnp.float32), 0.0)
    act = jnp.where(hot & inside, act.astype(jnp.float32), 0.0)
    cls = jnp.broadcast_to(jnp.sum(cls, axis=1, keepdims=True), (32, W))
    act = jnp.broadcast_to(jnp.sum(act, axis=1, keepdims=True), (32, W))
    gain = pick(cls, row_gains)
    tab[0, 8:40] = gain * act
    tab[1, 8:40] = act
    tab[2, 8:40] = gain
    tab[3, 8:40] = pick(cls, column_gains) * act
    tab[4, 8:40] = pick(cls, rate_gains) * act
    tab[1, 0:8] = jnp.zeros((8, W), jnp.float32)
    tab[2, 0:8] = jnp.zeros((8, W), jnp.float32)
    tab[5, 8:40] = 0.5 * (tab[2, 8:40] + tab[2, 7:39]) * tab[1, 8:40] * tab[1, 7:39]
    lanes = lax.broadcasted_iota(jnp.int32, (8, W), 1)
    sub = lax.broadcasted_iota(jnp.int32, (8, W), 0)
    first, last = lanes == 0, lanes == W - 1
    ends = jnp.where(first | last, 1.0, 2.0)
    for b in range(NBLK):

        def row(q, k):
            return jnp.broadcast_to(tab[q, 8 + k : 9 + k], (8, W))

        bu = jnp.where(sub == 0, row(5, b), row(0, b))
        bd = jnp.where(sub == 7, row(5, b + 1), row(0, b))
        cc, rr = row(3, b), row(4, b)
        for co, h, sc in ((cf, HF, SF), (cg, HG, SG)):
            at = slice(8 * b, 8 * b + 8)
            co[0, at] = (1.0 + h) - h * (bu + bd + cc * ends)
            co[1, at] = h * bu
            co[2, at] = h * bd
            co[3, at] = jnp.where(first, 0.0, h * cc)
            co[4, at] = jnp.where(last, 0.0, h * cc)
            co[5, at] = (h * h) * rr
            co[6, at] = 1.0 - (0.8 * h) * rr
            co[7, at] = (0.7 * h * h / sc) * rr
        if GHOST // BR <= b < (GHOST + HALF) // BR:
            mask[8 * b - GHOST : 8 * b - GHOST + 8] = row(1, b)

    def rescaled(src, dst, rows, ax, ay):
        at = slice(rows[0] + PAD, rows[1] + PAD)
        dst[0][at] = src[0][at] * ax
        dst[1][at] = src[1][at] * ay

    fine = [(fx.at[k], fy.at[k]) for k in range(2)]
    points = [(px.at[k], py.at[k]) for k in range(14)]
    shift = (dx, dy)
    chain = [(rx.at[k], ry.at[k]) for k in range(4)]
    fx[0, PAD : PAD + WIN] = uw[...] * (1.0 / SF)
    fy[0, PAD : PAD + WIN] = vw[...] * (HF / SF)
    g = 44
    for i in range(16):
        g -= 1
        step(fine[i % 2], fine[(i + 1) % 2], span(g), cf)
        if i == 7:
            rescaled(fine[0], points[0], span(g), CX, CY)
            rescaled(fine[0], chain[0], span(g), CX, CY)
    rescaled(fine[0], points[1], span(28), CX, CY)
    rescaled(fine[0], chain[1], span(28), CX, CY)
    step(points[0], shift, span(27), cg)
    lo, hi = (e + PAD for e in span(27))
    dx[lo:hi] = px[1, lo:hi] - dx[lo:hi]
    dy[lo:hi] = py[1, lo:hi] - dy[lo:hi]
    for i in range(16):
        if i < 12:
            step(points[i + 1], points[i + 2], span(27 - i), cg, shift)
        step(fine[i % 2], fine[(i + 1) % 2], span(27 - i), cf)
        if i == 7:
            rescaled(fine[0], chain[2], span(20), CX, CY)
    rescaled(fine[0], chain[3], span(12), CX, CY)

    lines = [(lx.at[k], ly.at[k]) for k in range(2)]
    for grp in (1, 2, 3):

        @pl.when(chip >= grp)
        def _():
            g = 31 - 4 * grp
            lo, hi = (e + PAD for e in span(g))
            for i in range(4):
                lx[0, i, lo:hi] = px[4 * grp - 2 + i, lo:hi] * (1.0 / CX)
                ly[0, i, lo:hi] = py[4 * grp - 2 + i, lo:hi] * (1.0 / CY)

            def two(_, c, rows):
                steps_of_lines(lines[0], lines[1], 4, rows, cf)
                steps_of_lines(lines[1], lines[0], 4, rows, cf)
                return c

            lax.fori_loop(0, 4, functools.partial(two, rows=span(g - 1)), 0)
            lo, hi = (e + PAD for e in span(g - 8))
            for i in range(4):
                lx[1, i, lo:hi] = lx[0, i, lo:hi] * CX
                ly[1, i, lo:hi] = ly[0, i, lo:hi] * CY
            steps_of_lines(lines[1], (ex, ey), 4, span(g - 9), cg)
            lax.fori_loop(0, 4, functools.partial(two, rows=span(g - 9)), 0)
            lo, hi = (e + PAD for e in span(g - 16))
            for i in range(4):
                ex[i, lo:hi] = lx[0, i, lo:hi] * CX - ex[i, lo:hi]
                ey[i, lo:hi] = ly[0, i, lo:hi] * CY - ey[i, lo:hi]
            for i in range(4):
                step(chain[(i + 3) % 4], chain[i], span(15 - 4 * grp - i), cg, (ex.at[i], ey.at[i]))

    live = mask[...] > 0.5
    mid = slice(PAD + GHOST, PAD + GHOST + HALF)
    mine = pl.ds(pl.multiple_of(HALF * core, 8), HALF)
    sends = []
    for i in range(2):
        k = 2 - 2 * core + i
        send[i, 0] = jnp.where(live, rx[k, mid] * SG, uw[GHOST : GHOST + HALF])
        send[i, 1] = jnp.where(live, ry[k, mid] * (SG / HG), vw[GHOST : GHOST + HALF])
        c = pltpu.make_async_remote_copy(
            src_ref=send.at[i], dst_ref=out_ref.at[i, :, mine], send_sem=xs.at[i], recv_sem=xr.at[i],
            device_id=mate, device_id_type=MESH,
        )
        c.start()
        sends.append(c)
    for i in range(2):
        k = 2 * core + i
        out_ref[i, 0, mine] = jnp.where(live, rx[k, mid] * SG, uw[GHOST : GHOST + HALF])
        out_ref[i, 1, mine] = jnp.where(live, ry[k, mid] * (SG / HG), vw[GHOST : GHOST + HALF])
    for c in sends:
        c.wait()


def local(initial_voltage, initial_recovery, block_class, block_active):
    f32, i32 = jnp.float32, jnp.int32
    full = PAD + WIN + PAD
    return pl.pallas_call(
        kernel,
        out_shape=jax.ShapeDtypeStruct((2, 2, ROWS, W), f32),
        in_specs=[pl.BlockSpec(memory_space=pl.ANY)] * 4,
        out_specs=pl.BlockSpec(memory_space=pltpu.VMEM),
        scratch_shapes=[
            pltpu.VMEM((WIN, W), f32),
            pltpu.VMEM((WIN, W), f32),
            *[pltpu.VMEM((1, 32), i32)] * 4,
            pltpu.VMEM((6, 48, W), f32),
            pltpu.VMEM((HALF, W), f32),
            *[pltpu.VMEM((8, WIN, W), f32)] * 2,
            *[pltpu.VMEM((2, full, W), f32)] * 2,
            *[pltpu.VMEM((14, full, W), f32)] * 2,
            *[pltpu.VMEM((full, W), f32)] * 2,
            *[pltpu.VMEM((2, 4, full, W), f32)] * 2,
            *[pltpu.VMEM((4, full, W), f32)] * 4,
            pltpu.VMEM((2, 2, HALF, W), f32),
            pltpu.SemaphoreType.DMA((4,)),
            pltpu.SemaphoreType.DMA((4,)),
            pltpu.SemaphoreType.DMA((4,)),
            pltpu.SemaphoreType.DMA((2,)),
            pltpu.SemaphoreType.DMA((2,)),
        ],
        compiler_params=pltpu.CompilerParams(
            collective_id=0, has_side_effects=True, vmem_limit_bytes=40 * 1024 * 1024
        ),
    )(initial_voltage, initial_recovery, block_class.reshape(1, 32), block_active.reshape(1, 32))


def solution(mesh):
    in_specs = (P("space", None), P("space", None), P("space"), P("space"))
    out_specs = P("tm", None, "space", None)
    return jax.shard_map(local, mesh=mesh, in_specs=in_specs, out_specs=out_specs, check_vma=False)
```

```python
import functools
import math

import jax
import jax.numpy as jnp
from jax import lax
from jax.experimental import pallas as pl
from jax.experimental.pallas import tpu as pltpu
from jax.sharding import PartitionSpec as P

MESH = pl.DeviceIdType.MESH


W = 128
BR = 8
ROWS = 256
HALF = 128
GHOST = 48
WIN = HALF + 2 * GHOST
NBLK = WIN // BR
PAD = 8
LOCAL = HALF + GHOST
SHARE = {0: 24, 1: 48, 2: 48, 3: 24}
OFFSET = {0: (0, 120), 1: (48, 48), 2: (96, 0), 3: (24, 96)}
SIDE = 24
REACH = 40
SENDS = [(a, b) for b in (1, 2, 3) for a in (0, 3, 1, 2) if a != b]
FIRST = 4
NL = 9

row_gains = (0.2, 0.35, 0.5, 0.6)
column_gains = (0.6, 0.5, 0.35, 0.2)
rate_gains = (0.06, 0.08, 0.1, 0.13)
HF = 0.05
HG = 0.05 * 8
SF = math.sqrt(3.0 / HF)
SG = math.sqrt(3.0 / HG)
CX = SF / SG
CY = (SF / HF) / (SG / HG)


def pick(classes, table):
    out = jnp.full_like(classes, table[3])
    for i in (2, 1, 0):
        out = jnp.where(classes == float(i), table[i], out)
    return out


def span(g, side=GHOST, rows=HALF):
    return (side - g) // 8 * 8, -(-(side + rows + g) // 8) * 8


def update(x, xu, xd, y, co):
    a0, bu, bd, cl, cr, h1, h2, h3 = co
    near = bu * xu + bd * xd
    side = cl * pltpu.roll(x, 1, 1) + cr * pltpu.roll(x, W - 1, 1)
    return (x * (a0 - x * x) - y + near) + side, h2 * y + (h1 * x + h3)


def step(src, dst, rows, co, extra=None):
    lo, hi = rows[0] + PAD, rows[1] + PAD
    sx, sy = src
    x = sx[lo:hi]
    nx, ny = update(x, sx[lo - 1 : hi - 1], sx[lo + 1 : hi + 1], sy[lo:hi], [co[q, rows[0] : rows[1]] for q in range(8)])
    if extra is not None:
        nx, ny = nx + extra[0][lo:hi], ny + extra[1][lo:hi]
    dst[0][lo:hi] = nx
    dst[1][lo:hi] = ny


def line_steps(bufs, spans, co, n):
    for m in range(n):
        for i, rows in enumerate(spans):
            src, dst = bufs[m % 2], bufs[(m + 1) % 2]
            step((src[0].at[i], src[1].at[i]), (dst[0].at[i], dst[1].at[i]), rows(m), co)


def kernel(
    u_ref, v_ref, cls_ref, act_ref, out_ref,
    uw, vw, ocls, oact, ncls, nact, tab, mask, cf, cg, fx, fy, px, py, dx, dy, lx, ly, ex, ey, rx, ry, send,
    sx, sy, tx, ty, qx, qy, wf, wg, sf, sg, part, rin,
    lsem, ssem, rsem, xs, xr, ps, pr, ready,
):
    t, s = lax.axis_index("tm"), lax.axis_index("space")
    chip, core = lax.div(t, 2), lax.rem(t, 2)
    up = lax.rem(s + 17 - 2 * core, 16)
    down = lax.rem(s + 15 + 2 * core, 16)
    to, fro = {"space": up}, {"space": down}
    sends_edge = s != 15 * (1 - core)
    takes_edge = s != 15 * core
    mate = {"tm": t + 1 - 2 * core}

    barrier = pltpu.get_barrier_semaphore()
    pl.semaphore_signal(barrier, inc=1, device_id=mate, device_id_type=MESH)

    @pl.when(takes_edge)
    def _():
        pl.semaphore_signal(barrier, inc=1, device_id=fro, device_id_type=MESH)

    for a, b in ((0, 1), (2, 1), (3, 1), (1, 2), (3, 2)):

        @pl.when(chip == a)
        def _(b=b):
            pl.semaphore_signal(barrier, inc=1, device_id={"tm": 2 * b + core}, device_id_type=MESH)

    here = pl.multiple_of(80 * core, 8)
    there = pl.multiple_of(GHOST * (1 - core), 8)
    local = [
        pltpu.make_async_copy(u_ref.at[pl.ds(here, LOCAL)], uw.at[pl.ds(there, LOCAL)], lsem.at[0]),
        pltpu.make_async_copy(v_ref.at[pl.ds(here, LOCAL)], vw.at[pl.ds(there, LOCAL)], lsem.at[1]),
        pltpu.make_async_copy(cls_ref, ocls, lsem.at[2]),
        pltpu.make_async_copy(act_ref, oact, lsem.at[3]),
    ]
    for c in local:
        c.start()
    for buf in (fx, fy):
        for k in range(2):
            buf[k, :PAD] = jnp.zeros((PAD, W), jnp.float32)
            buf[k, PAD + WIN :] = jnp.zeros((PAD, W), jnp.float32)

    pl.semaphore_wait(barrier, 1 + sends_edge.astype(jnp.int32) + jnp.where(chip == 1, 3, jnp.where(chip == 2, 2, 0)))
    edge = pl.multiple_of((ROWS - GHOST) * (1 - core), 8)
    land = pl.multiple_of(LOCAL * core, 8)
    edges = [
        (cls_ref, ncls),
        (act_ref, nact),
        (u_ref.at[pl.ds(edge, GHOST)], uw.at[pl.ds(land, GHOST)]),
        (v_ref.at[pl.ds(edge, GHOST)], vw.at[pl.ds(land, GHOST)]),
    ]
    remote = [
        pltpu.make_async_remote_copy(
            src_ref=a, dst_ref=b, send_sem=ssem.at[i], recv_sem=rsem.at[i], device_id=to, device_id_type=MESH
        )
        for i, (a, b) in enumerate(edges)
    ]

    @pl.when(sends_edge)
    def _():
        for c in remote:
            c.start()

    @pl.when(chip == 1)
    def _():
        for a in (0, 3):
            pl.semaphore_signal(ready, inc=1, device_id={"tm": 2 * a + core}, device_id_type=MESH)

    for c in local:
        c.wait()

    def tables(edges_here):
        wi = lax.broadcasted_iota(jnp.int32, (32, 32), 0) + (16 * core - GHOST // BR)
        lane = lax.broadcasted_iota(jnp.int32, (32, 32), 1)
        own = (wi >= 0) & (wi < 32)
        hot = lane == jnp.where(wi < 0, wi + 32, jnp.where(wi >= 32, wi - 32, wi))
        gi = wi + 32 * s
        inside = (gi >= 0) & (gi < 512)
        cls = jnp.broadcast_to(ocls[...], (32, 32))
        act = jnp.broadcast_to(oact[...], (32, 32))
        if edges_here:
            cls = jnp.where(own, cls, jnp.broadcast_to(ncls[...], (32, 32)))
            act = jnp.where(own, act, jnp.broadcast_to(nact[...], (32, 32)))
        cls = jnp.where(hot, cls.astype(jnp.float32), 0.0)
        act = jnp.where(hot & inside, act.astype(jnp.float32), 0.0)
        cls = jnp.broadcast_to(jnp.sum(cls, axis=1, keepdims=True), (32, W))
        act = jnp.broadcast_to(jnp.sum(act, axis=1, keepdims=True), (32, W))
        gain = pick(cls, row_gains)
        tab[0, 8:40] = gain * act
        tab[1, 8:40] = act
        tab[2, 8:40] = gain
        tab[3, 8:40] = pick(cls, column_gains) * act
        tab[4, 8:40] = pick(cls, rate_gains) * act
        tab[1, 0:8] = jnp.zeros((8, W), jnp.float32)
        tab[2, 0:8] = jnp.zeros((8, W), jnp.float32)
        tab[5, 8:40] = 0.5 * (tab[2, 8:40] + tab[2, 7:39]) * tab[1, 8:40] * tab[1, 7:39]
        lanes = lax.broadcasted_iota(jnp.int32, (8, W), 1)
        sub = lax.broadcasted_iota(jnp.int32, (8, W), 0)
        first, last = lanes == 0, lanes == W - 1
        ends = jnp.where(first | last, 1.0, 2.0)
        for b in range(NBLK):

            def row(q, k):
                return jnp.broadcast_to(tab[q, 8 + k : 9 + k], (8, W))

            bu = jnp.where(sub == 0, row(5, b), row(0, b))
            bd = jnp.where(sub == 7, row(5, b + 1), row(0, b))
            cc, rr = row(3, b), row(4, b)
            for co, h, sc in ((cf, HF, SF), (cg, HG, SG)):
                at = slice(8 * b, 8 * b + 8)
                co[0, at] = (1.0 + h) - h * (bu + bd + cc * ends)
                co[1, at] = h * bu
                co[2, at] = h * bd
                co[3, at] = jnp.where(first, 0.0, h * cc)
                co[4, at] = jnp.where(last, 0.0, h * cc)
                co[5, at] = (h * h) * rr
                co[6, at] = 1.0 - (0.8 * h) * rr
                co[7, at] = (0.7 * h * h / sc) * rr
            if GHOST // BR <= b < (GHOST + HALF) // BR:
                mask[8 * b - GHOST : 8 * b - GHOST + 8] = row(1, b)

    def rescaled(src, dst, rows, ax, ay):
        at = slice(rows[0] + PAD, rows[1] + PAD)
        dst[0][at] = src[0][at] * ax
        dst[1][at] = src[1][at] * ay

    fine = [(fx.at[k], fy.at[k]) for k in range(2)]
    points = [(px.at[k], py.at[k]) for k in range(14)]
    shift = (dx, dy)
    chain = [(rx.at[k], ry.at[k]) for k in range(4)]
    def prepare(span, ghost, last, co, cg):
        for i in range(16):
            step(fine[i % 2], fine[(i + 1) % 2], span(ghost - 1 - i), co)
            if i == 7:
                rescaled(fine[0], points[0], span(ghost - 8), CX, CY)
        rescaled(fine[0], points[1], span(ghost - 16), CX, CY)
        step(points[0], shift, span(ghost - 17), cg)
        lo, hi = (e + PAD for e in span(ghost - 17))
        dx[lo:hi] = px[1, lo:hi] - dx[lo:hi]
        dy[lo:hi] = py[1, lo:hi] - dy[lo:hi]
        go_on(span, ghost, 3, last, cg)

    def go_on(span, ghost, first, last, cg):
        for j in range(first, last + 1):
            step(points[j - 2], points[j - 1], span(ghost - 14 - j), cg, shift)

    def sending(a, b):
        at = pl.multiple_of(OFFSET[a][0] + (OFFSET[a][1] - OFFSET[a][0]) * core, 8)
        return pltpu.make_async_remote_copy(
            src_ref=part.at[b - 1, :, pl.ds(0, SHARE[a])], dst_ref=rin.at[:, pl.ds(at, SHARE[a])],
            send_sem=ps.at[b - 1], recv_sem=pr.at[a], device_id={"tm": 2 * b + core}, device_id_type=MESH,
        )

    def share(chips, at, sf, sg):
        n = SHARE[chips[0]]
        long = n + 2 * SIDE
        for i in range(NL):
            sx[0, i, PAD : PAD + long] = px[i + 1, pl.ds(at, long)] * (1.0 / CX)
            sy[0, i, PAD : PAD + long] = py[i + 1, pl.ds(at, long)] * (1.0 / CY)
        rows = functools.partial(span, side=SIDE, rows=n)
        lines = [(sx.at[k], sy.at[k]) for k in range(2)]
        line_steps(lines, [lambda m, i=i: rows(23 - i - m) for i in range(NL)], sf, 8)
        for i in range(1, NL):
            rescaled((sx.at[0, i], sy.at[0, i]), (sx.at[1, i], sy.at[1, i]), rows(16 - i), CX, CY)
            step((sx.at[1, i], sy.at[1, i]), (qx.at[i], qy.at[i]), rows(8 - i), sg)
        line_steps(lines, [lambda m, i=i: rows(15 - i - m) for i in range(NL)], sf, 8)
        rescaled((sx.at[0, 0], sy.at[0, 0]), (tx.at[0], ty.at[0]), rows(8), CX, CY)
        for i in range(1, NL):
            lo, hi = (e + PAD for e in rows(8 - i))
            qx[i, lo:hi] = sx[0, i, lo:hi] * CX - qx[i, lo:hi]
            qy[i, lo:hi] = sy[0, i, lo:hi] * CY - qy[i, lo:hi]
        mid = slice(PAD + SIDE, PAD + SIDE + n)
        for i in range(NL):
            if i:
                step((tx.at[i - 1], ty.at[i - 1]), (tx.at[i], ty.at[i]), rows(8 - i), sg, (qx.at[i], qy.at[i]))
            if i % 4 == 0:
                b = i // 4 + 1
                part[b - 1, 0, 0:n] = tx[i, mid]
                part[b - 1, 1, 0:n] = ty[i, mid]
                if i == 0 and 0 in chips:
                    pl.semaphore_wait(ready, 1)
                for a in chips:

                    @pl.when(chip == a)
                    def _(a=a, b=b):
                        if a != b:
                            sending(a, b).start()
                        else:
                            own = pl.multiple_of(OFFSET[a][0] + (OFFSET[a][1] - OFFSET[a][0]) * core, 8)
                            rin[:, pl.ds(own, n)] = part[b - 1, :, 0:n]

    def offset(a, b):
        x = jnp.where(chip == a, OFFSET[a][0], OFFSET[b][0])
        y = jnp.where(chip == a, OFFSET[a][1], OFFSET[b][1])
        return GHOST - 8 + jnp.where(core == 0, x, y)

    @pl.when((chip == 1) | (chip == 2))
    def _():
        tables(False)
        n = SHARE[1]
        long = n + 2 * REACH
        base = pl.multiple_of(offset(1, 2) - REACH, 8)
        for q in range(8):
            wf[q] = cf[q, pl.ds(base, long)]
            wg[q] = cg[q, pl.ds(base, long)]
            sf[q] = cf[q, pl.ds(pl.multiple_of(base + REACH - SIDE, 8), n + 2 * SIDE)]
            sg[q] = cg[q, pl.ds(pl.multiple_of(base + REACH - SIDE, 8), n + 2 * SIDE)]
        fx[0, PAD : PAD + long] = uw[pl.ds(base, long)] * (1.0 / SF)
        fy[0, PAD : PAD + long] = vw[pl.ds(base, long)] * (HF / SF)
        prepare(functools.partial(span, side=REACH, rows=n), REACH, 10, wf, wg)
        share((1, 2), PAD + REACH - SIDE, sf, sg)

    @pl.when(takes_edge)
    def _():
        for c in remote:
            c.wait_recv()

    @pl.when(jnp.logical_not(takes_edge))
    def _():
        uw[pl.ds(land, GHOST)] = jnp.zeros((GHOST, W), jnp.float32)
        vw[pl.ds(land, GHOST)] = jnp.zeros((GHOST, W), jnp.float32)
        ncls[...] = jnp.zeros((1, 32), jnp.int32)
        nact[...] = jnp.zeros((1, 32), jnp.int32)

    tables(True)
    fx[0, PAD : PAD + WIN] = uw[...] * (1.0 / SF)
    fy[0, PAD : PAD + WIN] = vw[...] * (HF / SF)
    prepare(span, GHOST, 6, cf, cg)

    @pl.when(chip != 1)
    def _():
        go_on(span, GHOST, 7, 10, cg)

    @pl.when((chip == 0) | (chip == 3))
    def _():
        n = SHARE[0]
        base = pl.multiple_of(offset(0, 3) - SIDE, 8)
        for q in range(8):
            sf[q, 0 : n + 2 * SIDE] = cf[q, pl.ds(base, n + 2 * SIDE)]
            sg[q, 0 : n + 2 * SIDE] = cg[q, pl.ds(base, n + 2 * SIDE)]
        share((0, 3), pl.multiple_of(base + PAD, 8), sf, sg)

    @pl.when(chip == 0)
    def _():
        for i in range(16):
            step(fine[i % 2], fine[(i + 1) % 2], span(15 - i), cf)
            if i == 7:
                rescaled(fine[0], chain[2], span(0), CX, CY)
        rescaled(fine[0], chain[3], span(0), CX, CY)
        for k in range(2):
            rescaled(points[k], chain[k], span(0), 1.0, 1.0)

    @pl.when(chip == 3)
    def _():
        go_on(span, GHOST, 11, 14, cg)

    @pl.when(chip > 0)
    def _():
        lines = [(lx.at[k], ly.at[k]) for k in range(2)]
        lo, hi = (e + PAD for e in span(19))
        for i in range(4):
            k = 4 * chip - 2 + i
            lx[0, i, lo:hi] = px[k, lo:hi] * (1.0 / CX)
            ly[0, i, lo:hi] = py[k, lo:hi] * (1.0 / CY)
        line_steps(lines, [lambda m, i=i: span(18 - i - m) for i in range(4)], cf, 8)
        for i in range(4):
            rescaled((lx.at[0, i], ly.at[0, i]), (lx.at[1, i], ly.at[1, i]), span(11 - i), CX, CY)
            step((lx.at[1, i], ly.at[1, i]), (ex.at[i], ey.at[i]), span(3 - i), cg)
        line_steps(lines, [lambda m, i=i: span(10 - i - m) for i in range(4)], cf, 8)
        for i in range(4):
            lo, hi = (e + PAD for e in span(3 - i))
            ex[i, lo:hi] = lx[0, i, lo:hi] * CX - ex[i, lo:hi]
            ey[i, lo:hi] = ly[0, i, lo:hi] * CY - ey[i, lo:hi]
        for a in range(4):

            @pl.when(chip != a)
            def _(a=a):
                sending(a, 1).wait_recv()

        at = slice(PAD + GHOST - 8, PAD + GHOST + HALF + 8)
        rx[3, at] = rin[0]
        ry[3, at] = rin[1]
        for i in range(4):
            step(chain[(i + 3) % 4], chain[i], span(3 - i), cg, (ex.at[i], ey.at[i]))

    live = mask[...] > 0.5
    mid = slice(PAD + GHOST, PAD + GHOST + HALF)
    mine = pl.ds(pl.multiple_of(HALF * core, 8), HALF)
    sends = []
    for i in range(2):
        k = 2 - 2 * core + i
        send[i, 0] = jnp.where(live, rx[k, mid] * SG, uw[GHOST : GHOST + HALF])
        send[i, 1] = jnp.where(live, ry[k, mid] * (SG / HG), vw[GHOST : GHOST + HALF])
        c = pltpu.make_async_remote_copy(
            src_ref=send.at[i], dst_ref=out_ref.at[i, :, mine], send_sem=xs.at[i], recv_sem=xr.at[i],
            device_id=mate, device_id_type=MESH,
        )
        c.start()
        sends.append(c)
    for i in range(2):
        k = 2 * core + i
        out_ref[i, 0, mine] = jnp.where(live, rx[k, mid] * SG, uw[GHOST : GHOST + HALF])
        out_ref[i, 1, mine] = jnp.where(live, ry[k, mid] * (SG / HG), vw[GHOST : GHOST + HALF])
    for c in sends:
        c.wait()
    for a, b in SENDS:

        @pl.when(chip == a)
        def _(a=a, b=b):
            sending(a, b).wait_send()

    @pl.when(sends_edge)
    def _():
        for c in remote:
            c.wait_send()


def local(initial_voltage, initial_recovery, block_class, block_active):
    f32, i32 = jnp.float32, jnp.int32
    given = (initial_voltage, initial_recovery, block_class.reshape(1, 32), block_active.reshape(1, 32))
    given = [pltpu.with_memory_space_constraint(x, pltpu.HBM) for x in given]
    full = PAD + WIN + PAD
    share = PAD + SHARE[1] + 2 * SIDE + PAD
    return pl.pallas_call(
        kernel,
        out_shape=jax.ShapeDtypeStruct((2, 2, ROWS, W), f32),
        in_specs=[pl.BlockSpec(memory_space=pltpu.HBM)] * 4,
        out_specs=pl.BlockSpec(memory_space=pltpu.VMEM),
        scratch_shapes=[
            pltpu.VMEM((WIN, W), f32),
            pltpu.VMEM((WIN, W), f32),
            *[pltpu.VMEM((1, 32), i32)] * 4,
            pltpu.VMEM((6, 48, W), f32),
            pltpu.VMEM((HALF, W), f32),
            *[pltpu.VMEM((8, WIN, W), f32)] * 2,
            *[pltpu.VMEM((2, full, W), f32)] * 2,
            *[pltpu.VMEM((14, full, W), f32)] * 2,
            *[pltpu.VMEM((full, W), f32)] * 2,
            *[pltpu.VMEM((2, 4, full, W), f32)] * 2,
            *[pltpu.VMEM((4, full, W), f32)] * 4,
            pltpu.VMEM((2, 2, HALF, W), f32),
            *[pltpu.VMEM((2, NL, share, W), f32)] * 2,
            *[pltpu.VMEM((NL, share, W), f32)] * 4,
            *[pltpu.VMEM((8, SHARE[1] + 2 * REACH, W), f32)] * 2,
            *[pltpu.VMEM((8, SHARE[1] + 2 * SIDE, W), f32)] * 2,
            pltpu.VMEM((3, 2, SHARE[1], W), f32),
            pltpu.VMEM((2, 144, W), f32),
            pltpu.SemaphoreType.DMA((4,)),
            pltpu.SemaphoreType.DMA((4,)),
            pltpu.SemaphoreType.DMA((4,)),
            pltpu.SemaphoreType.DMA((2,)),
            pltpu.SemaphoreType.DMA((2,)),
            pltpu.SemaphoreType.DMA((3,)),
            pltpu.SemaphoreType.DMA((4,)),
            pltpu.SemaphoreType.REGULAR,
        ],
        compiler_params=pltpu.CompilerParams(
            collective_id=0, has_side_effects=True, vmem_limit_bytes=40 * 1024 * 1024
        ),
    )(*given)


def solution(mesh):
    in_specs = (P("space", None), P("space", None), P("space"), P("space"))
    out_specs = P("tm", None, "space", None)
    return jax.shard_map(local, mesh=mesh, in_specs=in_specs, out_specs=out_specs, check_vma=False)
```

```python
import functools
import math

import jax
import jax.numpy as jnp
from jax import lax
from jax.experimental import pallas as pl
from jax.experimental.pallas import tpu as pltpu
from jax.sharding import PartitionSpec as P

MESH = pl.DeviceIdType.MESH


W = 128
BR = 8
ROWS = 256
HALF = 128
GHOST = 48
WIN = HALF + 2 * GHOST
NBLK = WIN // BR
PAD = 8
LOCAL = HALF + GHOST
SHARE = 48
SIDE = 24
REACH = 40
SENDS = [(a, b) for b in (1, 2, 3) for a in (0, 1, 2) if a != b]
FIRST = 4
NL = 9

row_gains = (0.2, 0.35, 0.5, 0.6)
column_gains = (0.6, 0.5, 0.35, 0.2)
rate_gains = (0.06, 0.08, 0.1, 0.13)
HF = 0.05
HG = 0.05 * 8
SF = math.sqrt(3.0 / HF)
SG = math.sqrt(3.0 / HG)
CX = SF / SG
CY = (SF / HF) / (SG / HG)


def pick(classes, table):
    out = jnp.full_like(classes, table[3])
    for i in (2, 1, 0):
        out = jnp.where(classes == float(i), table[i], out)
    return out


def span(g, side=GHOST, rows=HALF):
    return (side - g) // 8 * 8, -(-(side + rows + g) // 8) * 8


def update(x, xu, xd, y, co):
    a0, bu, bd, cl, cr, h1, h2, h3 = co
    near = bu * xu + bd * xd
    side = cl * pltpu.roll(x, 1, 1) + cr * pltpu.roll(x, W - 1, 1)
    return (x * (a0 - x * x) - y + near) + side, h2 * y + (h1 * x + h3)


def step(src, dst, rows, co, extra=None, chunk=32):
    sx, sy = src
    for r in range(rows[0], rows[1], chunk):
        end = min(r + chunk, rows[1])
        lo, hi = r + PAD, end + PAD
        c = [co[q, r:end] for q in range(8)]
        nx, ny = update(sx[lo:hi], sx[lo - 1 : hi - 1], sx[lo + 1 : hi + 1], sy[lo:hi], c)
        if extra is not None:
            nx, ny = nx + extra[0][lo:hi], ny + extra[1][lo:hi]
        dst[0][lo:hi] = nx
        dst[1][lo:hi] = ny


def line_steps(jobs, co, chunk=16):
    first = min((rows[0] for _, _, rows in jobs), default=0)
    last = max((rows[1] for _, _, rows in jobs), default=0)
    for r in range(first, last, chunk):
        for src, dst, (lo, hi) in jobs:
            part = max(lo, r), min(hi, r + chunk)
            if part[0] < part[1]:
                step(src, dst, part, co, chunk=chunk)


def kernel(
    u_ref, v_ref, cls_ref, act_ref, out_ref,
    uw, vw, ocls, oact, ncls, nact, tab, mask, cf, cg, fx, fy, px, py, dx, dy, lx, ly, ex, ey, rx, ry, send,
    sx, sy, tx, ty, qx, qy, wf, wg, sf, sg, part, rin,
    lsem, ssem, rsem, xs, xr, ps, pr, ready,
):
    t, s = lax.axis_index("tm"), lax.axis_index("space")
    chip, core = lax.div(t, 2), lax.rem(t, 2)
    up = lax.rem(s + 17 - 2 * core, 16)
    down = lax.rem(s + 15 + 2 * core, 16)
    to, fro = {"space": up}, {"space": down}
    sends_edge = s != 15 * (1 - core)
    takes_edge = s != 15 * core
    mate = {"tm": t + 1 - 2 * core}

    barrier = pltpu.get_barrier_semaphore()
    pl.semaphore_signal(barrier, inc=1, device_id=mate, device_id_type=MESH)

    @pl.when(takes_edge)
    def _():
        pl.semaphore_signal(barrier, inc=1, device_id=fro, device_id_type=MESH)

    for a, b in ((0, 1), (2, 1), (3, 1), (1, 2), (3, 2)):

        @pl.when(chip == a)
        def _(b=b):
            pl.semaphore_signal(barrier, inc=1, device_id={"tm": 2 * b + core}, device_id_type=MESH)

    here = pl.multiple_of(80 * core, 8)
    there = pl.multiple_of(GHOST * (1 - core), 8)
    local = [
        pltpu.make_async_copy(u_ref.at[pl.ds(here, LOCAL)], uw.at[pl.ds(there, LOCAL)], lsem.at[0]),
        pltpu.make_async_copy(v_ref.at[pl.ds(here, LOCAL)], vw.at[pl.ds(there, LOCAL)], lsem.at[1]),
        pltpu.make_async_copy(cls_ref, ocls, lsem.at[2]),
        pltpu.make_async_copy(act_ref, oact, lsem.at[3]),
    ]
    for c in local:
        c.start()
    for buf in (fx, fy):
        for k in range(2):
            buf[k, :PAD] = jnp.zeros((PAD, W), jnp.float32)
            buf[k, PAD + WIN :] = jnp.zeros((PAD, W), jnp.float32)

    def tables(edges_here):
        wi = lax.broadcasted_iota(jnp.int32, (32, 32), 0) + (16 * core - GHOST // BR)
        lane = lax.broadcasted_iota(jnp.int32, (32, 32), 1)
        own = (wi >= 0) & (wi < 32)
        hot = lane == jnp.where(wi < 0, wi + 32, jnp.where(wi >= 32, wi - 32, wi))
        gi = wi + 32 * s
        inside = (gi >= 0) & (gi < 512)
        cls = jnp.broadcast_to(ocls[...], (32, 32))
        act = jnp.broadcast_to(oact[...], (32, 32))
        if edges_here:
            cls = jnp.where(own, cls, jnp.broadcast_to(ncls[...], (32, 32)))
            act = jnp.where(own, act, jnp.broadcast_to(nact[...], (32, 32)))
        cls = jnp.where(hot, cls.astype(jnp.float32), 0.0)
        act = jnp.where(hot & inside, act.astype(jnp.float32), 0.0)
        cls = jnp.broadcast_to(jnp.sum(cls, axis=1, keepdims=True), (32, W))
        act = jnp.broadcast_to(jnp.sum(act, axis=1, keepdims=True), (32, W))
        gain = pick(cls, row_gains)
        tab[0, 8:40] = gain * act
        tab[1, 8:40] = act
        tab[2, 8:40] = gain
        tab[3, 8:40] = pick(cls, column_gains) * act
        tab[4, 8:40] = pick(cls, rate_gains) * act
        tab[1, 0:8] = jnp.zeros((8, W), jnp.float32)
        tab[2, 0:8] = jnp.zeros((8, W), jnp.float32)
        tab[5, 8:40] = 0.5 * (tab[2, 8:40] + tab[2, 7:39]) * tab[1, 8:40] * tab[1, 7:39]
        lanes = lax.broadcasted_iota(jnp.int32, (8, W), 1)
        sub = lax.broadcasted_iota(jnp.int32, (8, W), 0)
        first, last = lanes == 0, lanes == W - 1
        ends = jnp.where(first | last, 1.0, 2.0)
        for b in range(NBLK):

            def row(q, k):
                return jnp.broadcast_to(tab[q, 8 + k : 9 + k], (8, W))

            bu = jnp.where(sub == 0, row(5, b), row(0, b))
            bd = jnp.where(sub == 7, row(5, b + 1), row(0, b))
            cc, rr = row(3, b), row(4, b)
            for co, h, sc in ((cf, HF, SF), (cg, HG, SG)):
                at = slice(8 * b, 8 * b + 8)
                co[0, at] = (1.0 + h) - h * (bu + bd + cc * ends)
                co[1, at] = h * bu
                co[2, at] = h * bd
                co[3, at] = jnp.where(first, 0.0, h * cc)
                co[4, at] = jnp.where(last, 0.0, h * cc)
                co[5, at] = (h * h) * rr
                co[6, at] = 1.0 - (0.8 * h) * rr
                co[7, at] = (0.7 * h * h / sc) * rr
            if GHOST // BR <= b < (GHOST + HALF) // BR:
                mask[8 * b - GHOST : 8 * b - GHOST + 8] = row(1, b)

    def rescaled(src, dst, rows, ax, ay):
        at = slice(rows[0] + PAD, rows[1] + PAD)
        dst[0][at] = src[0][at] * ax
        dst[1][at] = src[1][at] * ay

    fine = [(fx.at[k], fy.at[k]) for k in range(2)]
    points = [(px.at[k], py.at[k]) for k in range(14)]
    shift = (dx, dy)
    chain = [(rx.at[k], ry.at[k]) for k in range(4)]
    def prepare(span, ghost, last, co, cg):
        for i in range(16):
            step(fine[i % 2], fine[(i + 1) % 2], span(ghost - 1 - i), co)
            if i == 7:
                rescaled(fine[0], points[0], span(ghost - 8), CX, CY)
        rescaled(fine[0], points[1], span(ghost - 16), CX, CY)
        step(points[0], shift, span(ghost - 17), cg)
        lo, hi = (e + PAD for e in span(ghost - 17))
        dx[lo:hi] = px[1, lo:hi] - dx[lo:hi]
        dy[lo:hi] = py[1, lo:hi] - dy[lo:hi]
        go_on(span, ghost, 3, last, cg)

    def go_on(span, ghost, first, last, cg):
        for j in range(first, last + 1):
            step(points[j - 2], points[j - 1], span(ghost - 14 - j), cg, shift)

    def begins(a):
        return pl.multiple_of(SHARE * (a + (2 - 2 * a) * core), 8)

    def sending(a, b):
        return pltpu.make_async_remote_copy(
            src_ref=part.at[b - 1], dst_ref=rin.at[:, pl.ds(begins(a), SHARE)], send_sem=ps.at[b - 1], recv_sem=pr.at[a],
            device_id={"tm": 2 * b + core}, device_id_type=MESH,
        )

    wide = functools.partial(span, side=REACH, rows=SHARE)

    def share_begins():
        base = pl.multiple_of(GHOST - 8 - REACH + begins(chip), 8)
        long = SHARE + 2 * REACH
        inner = pl.multiple_of(base + REACH - SIDE, 8)
        for q in range(8):
            wf[q] = cf[q, pl.ds(base, long)]
            wg[q] = cg[q, pl.ds(base, long)]
            sf[q] = cf[q, pl.ds(inner, SHARE + 2 * SIDE)]
            sg[q] = cg[q, pl.ds(inner, SHARE + 2 * SIDE)]
        fx[0, PAD : PAD + long] = uw[pl.ds(base, long)] * (1.0 / SF)
        fy[0, PAD : PAD + long] = vw[pl.ds(base, long)] * (HF / SF)
        prepare(wide, REACH, 2, wf, wg)

    def share():
        at = slice(PAD + REACH - SIDE, PAD + REACH + SHARE + SIDE)
        own = slice(PAD, PAD + SHARE + 2 * SIDE)
        mid = slice(PAD + SIDE, PAD + SIDE + SHARE)
        rows = functools.partial(span, side=SIDE, rows=SHARE)

        def line(m, i):
            return sx.at[m % 2, i], sy.at[m % 2, i]

        def link(i):
            return tx.at[i], ty.at[i]

        for tick in range(16 + 2 * NL):
            if 0 <= tick < NL - 1:
                go_on(wide, REACH, tick + 3, tick + 3, wg)
            if 0 <= tick < NL:
                sx[0, tick, own] = px[tick + 1, at] * (1.0 / CX)
                sy[0, tick, own] = py[tick + 1, at] * (1.0 / CY)
            i = tick - 16
            if 0 <= i < NL:
                if i == 0:
                    rescaled(line(0, 0), link(0), rows(8), CX, CY)
                else:
                    lo, hi = (e + PAD for e in rows(8 - i))
                    qx[i, lo:hi] = sx[0, i, lo:hi] * CX - qx[i, lo:hi]
                    qy[i, lo:hi] = sy[0, i, lo:hi] * CY - qy[i, lo:hi]
                    step(link(i - 1), link(i), rows(8 - i), sg, (qx.at[i], qy.at[i]))
                if i % 4 == 0:
                    b = i // 4
                    part[b, 0] = tx[i, mid]
                    part[b, 1] = ty[i, mid]
            line_steps(
                [
                    (line(m, i), line(m + 1, i), rows(23 - i - m))
                    for i in range(NL)
                    for m in (tick - i,)
                    if 0 <= m < 16
                ],
                sf,
            )
            i = tick - 7
            if 1 <= i < NL:
                rescaled(line(0, i), line(1, i), rows(16 - i), CX, CY)
                step(line(1, i), (qx.at[i], qy.at[i]), rows(8 - i), sg)

            i = tick - 16
            if i in (0, 4, 8):

                @pl.when(chip == 0)
                def _():
                    if i == 0:
                        pl.semaphore_wait(ready, 1)

                b = i // 4 + 1
                for a in range(3):

                    @pl.when(chip == a)
                    def _(a=a, b=b):
                        if a != b:
                            sending(a, b).start()
                        else:
                            rin[:, pl.ds(begins(a), SHARE)] = part[b - 1]

    @pl.when((chip == 1) | (chip == 2))
    def _():
        for c in local:
            c.wait()
        tables(False)
        share_begins()

    pl.semaphore_wait(barrier, 1 + sends_edge.astype(jnp.int32) + jnp.where(chip == 1, 3, jnp.where(chip == 2, 2, 0)))
    edge = pl.multiple_of((ROWS - GHOST) * (1 - core), 8)
    land = pl.multiple_of(LOCAL * core, 8)
    edges = [
        (u_ref.at[pl.ds(edge, GHOST)], uw.at[pl.ds(land, GHOST)]),
        (v_ref.at[pl.ds(edge, GHOST)], vw.at[pl.ds(land, GHOST)]),
        (cls_ref, ncls),
        (act_ref, nact),
    ]
    remote = [
        pltpu.make_async_remote_copy(
            src_ref=a, dst_ref=b, send_sem=ssem.at[i], recv_sem=rsem.at[i], device_id=to, device_id_type=MESH
        )
        for i, (a, b) in enumerate(edges)
    ]

    @pl.when(sends_edge)
    def _():
        for c in remote:
            c.start()

    @pl.when(chip == 1)
    def _():
        pl.semaphore_signal(ready, inc=1, device_id={"tm": core}, device_id_type=MESH)

    @pl.when((chip == 0) | (chip == 3))
    def _():
        for c in local:
            c.wait()

    def edges_in():
        @pl.when(takes_edge)
        def _():
            for c in remote:
                c.wait_recv()

        @pl.when(jnp.logical_not(takes_edge))
        def _():
            uw[pl.ds(land, GHOST)] = jnp.zeros((GHOST, W), jnp.float32)
            vw[pl.ds(land, GHOST)] = jnp.zeros((GHOST, W), jnp.float32)
            ncls[...] = jnp.zeros((1, 32), jnp.int32)
            nact[...] = jnp.zeros((1, 32), jnp.int32)

        tables(True)

    @pl.when(chip == 0)
    def _():
        edges_in()
        share_begins()

    @pl.when(chip < 3)
    def _():
        share()

    @pl.when(chip > 0)
    def _():
        edges_in()

    fx[0, PAD : PAD + WIN] = uw[...] * (1.0 / SF)
    fy[0, PAD : PAD + WIN] = vw[...] * (HF / SF)

    @pl.when(chip == 0)
    def _():
        for i in range(32):
            step(fine[i % 2], fine[(i + 1) % 2], span(31 - i), cf)
            if i % 8 == 7:
                rescaled(fine[0], chain[i // 8], span(0), CX, CY)

    @pl.when(chip > 0)
    def _():
        prepare(span, GHOST, 6, cf, cg)

    @pl.when(chip > 1)
    def _():
        go_on(span, GHOST, 7, 10, cg)

    @pl.when(chip == 3)
    def _():
        go_on(span, GHOST, 11, 14, cg)

    @pl.when(chip > 0)
    def _():
        lo, hi = (e + PAD for e in span(19))
        for i in range(4):
            k = 4 * chip - 2 + i
            lx[0, i, lo:hi] = px[k, lo:hi] * (1.0 / CX)
            ly[0, i, lo:hi] = py[k, lo:hi] * (1.0 / CY)
        for m in range(16):
            if m == 8:
                for i in range(4):
                    rescaled((lx.at[0, i], ly.at[0, i]), (lx.at[1, i], ly.at[1, i]), span(11 - i), CX, CY)
                    step((lx.at[1, i], ly.at[1, i]), (ex.at[i], ey.at[i]), span(3 - i), cg)
            a, b = m % 2, (m + 1) % 2
            line_steps(
                [((lx.at[a, i], ly.at[a, i]), (lx.at[b, i], ly.at[b, i]), span(18 - i - m)) for i in range(4)], cf
            )
        for i in range(4):
            lo, hi = (e + PAD for e in span(3 - i))
            ex[i, lo:hi] = lx[0, i, lo:hi] * CX - ex[i, lo:hi]
            ey[i, lo:hi] = ly[0, i, lo:hi] * CY - ey[i, lo:hi]
        for a in range(3):

            @pl.when(chip != a)
            def _(a=a):
                sending(a, 1).wait_recv()

        at = slice(PAD + GHOST - 8, PAD + GHOST + HALF + 8)
        rx[3, at] = rin[0]
        ry[3, at] = rin[1]
        for i in range(4):
            step(chain[(i + 3) % 4], chain[i], span(3 - i), cg, (ex.at[i], ey.at[i]))

    live = mask[...] > 0.5
    mid = slice(PAD + GHOST, PAD + GHOST + HALF)
    mine = pl.ds(pl.multiple_of(HALF * core, 8), HALF)
    sends = []
    for i in range(2):
        k = 2 - 2 * core + i
        send[i, 0] = jnp.where(live, rx[k, mid] * SG, uw[GHOST : GHOST + HALF])
        send[i, 1] = jnp.where(live, ry[k, mid] * (SG / HG), vw[GHOST : GHOST + HALF])
        c = pltpu.make_async_remote_copy(
            src_ref=send.at[i], dst_ref=out_ref.at[i, :, mine], send_sem=xs.at[i], recv_sem=xr.at[i],
            device_id=mate, device_id_type=MESH,
        )
        c.start()
        sends.append(c)
    for i in range(2):
        k = 2 * core + i
        out_ref[i, 0, mine] = jnp.where(live, rx[k, mid] * SG, uw[GHOST : GHOST + HALF])
        out_ref[i, 1, mine] = jnp.where(live, ry[k, mid] * (SG / HG), vw[GHOST : GHOST + HALF])
    for c in sends:
        c.wait()
    for a, b in SENDS:

        @pl.when(chip == a)
        def _(a=a, b=b):
            sending(a, b).wait_send()

    @pl.when(sends_edge)
    def _():
        for c in remote:
            c.wait_send()


def local(initial_voltage, initial_recovery, block_class, block_active):
    f32, i32 = jnp.float32, jnp.int32
    given = (initial_voltage, initial_recovery, block_class.reshape(1, 32), block_active.reshape(1, 32))
    given = [pltpu.with_memory_space_constraint(x, pltpu.HBM) for x in given]
    full = PAD + WIN + PAD
    share = PAD + SHARE + 2 * SIDE + PAD
    return pl.pallas_call(
        kernel,
        out_shape=jax.ShapeDtypeStruct((2, 2, ROWS, W), f32),
        in_specs=[pl.BlockSpec(memory_space=pltpu.HBM)] * 4,
        out_specs=pl.BlockSpec(memory_space=pltpu.VMEM),
        scratch_shapes=[
            pltpu.VMEM((WIN, W), f32),
            pltpu.VMEM((WIN, W), f32),
            *[pltpu.VMEM((1, 32), i32)] * 4,
            pltpu.VMEM((6, 48, W), f32),
            pltpu.VMEM((HALF, W), f32),
            *[pltpu.VMEM((8, WIN, W), f32)] * 2,
            *[pltpu.VMEM((2, full, W), f32)] * 2,
            *[pltpu.VMEM((14, full, W), f32)] * 2,
            *[pltpu.VMEM((full, W), f32)] * 2,
            *[pltpu.VMEM((2, 4, full, W), f32)] * 2,
            *[pltpu.VMEM((4, full, W), f32)] * 4,
            pltpu.VMEM((2, 2, HALF, W), f32),
            *[pltpu.VMEM((2, NL, share, W), f32)] * 2,
            *[pltpu.VMEM((NL, share, W), f32)] * 4,
            *[pltpu.VMEM((8, SHARE + 2 * REACH, W), f32)] * 2,
            *[pltpu.VMEM((8, SHARE + 2 * SIDE, W), f32)] * 2,
            pltpu.VMEM((3, 2, SHARE, W), f32),
            pltpu.VMEM((2, 144, W), f32),
            pltpu.SemaphoreType.DMA((4,)),
            pltpu.SemaphoreType.DMA((4,)),
            pltpu.SemaphoreType.DMA((4,)),
            pltpu.SemaphoreType.DMA((2,)),
            pltpu.SemaphoreType.DMA((2,)),
            pltpu.SemaphoreType.DMA((3,)),
            pltpu.SemaphoreType.DMA((3,)),
            pltpu.SemaphoreType.REGULAR,
        ],
        compiler_params=pltpu.CompilerParams(
            collective_id=0, has_side_effects=True, vmem_limit_bytes=40 * 1024 * 1024
        ),
    )(*given)


def solution(mesh):
    in_specs = (P("space", None), P("space", None), P("space"), P("space"))
    out_specs = P("tm", None, "space", None)
    return jax.shard_map(local, mesh=mesh, in_specs=in_specs, out_specs=out_specs, check_vma=False)
```

```python
import functools
import math

import jax
import jax.numpy as jnp
from jax import lax
from jax.experimental import pallas as pl
from jax.experimental.pallas import tpu as pltpu
from jax.sharding import PartitionSpec as P

MESH = pl.DeviceIdType.MESH


W = 128
BR = 8
ROWS = 256
HALF = 128
GHOST = 48
WIN = HALF + 2 * GHOST
NBLK = WIN // BR
PAD = 8
LOCAL = HALF + GHOST
SHARE = 48
SIDE = 24
OWN = 44
REACH = 40
SENDS = [(a, b) for b in (1, 2, 3) for a in (0, 1, 2) if a != b]
FIRST = 4
NL = 9

row_gains = (0.2, 0.35, 0.5, 0.6)
column_gains = (0.6, 0.5, 0.35, 0.2)
rate_gains = (0.06, 0.08, 0.1, 0.13)
HF = 0.05
HG = 0.05 * 8
SF = math.sqrt(3.0 / HF)
SG = math.sqrt(3.0 / HG)
CX = SF / SG
CY = (SF / HF) / (SG / HG)


def pick(classes, table):
    out = jnp.full_like(classes, table[3])
    for i in (2, 1, 0):
        out = jnp.where(classes == float(i), table[i], out)
    return out


def span(g, side=GHOST, rows=HALF):
    return (side - g) // 8 * 8, -(-(side + rows + g) // 8) * 8


def update(x, xu, xd, y, co):
    a0, bu, bd, cl, cr, h1, h2, h3 = co
    near = bu * xu + bd * xd
    side = cl * pltpu.roll(x, 1, 1) + cr * pltpu.roll(x, W - 1, 1)
    return (x * (a0 - x * x) - y + near) + side, h2 * y + (h1 * x + h3)


def step(src, dst, rows, co, extra=None, chunk=32):
    sx, sy = src
    for r in range(rows[0], rows[1], chunk):
        end = min(r + chunk, rows[1])
        lo, hi = r + PAD, end + PAD
        c = [co[q, r:end] for q in range(8)]
        nx, ny = update(sx[lo:hi], sx[lo - 1 : hi - 1], sx[lo + 1 : hi + 1], sy[lo:hi], c)
        if extra is not None:
            nx, ny = nx + extra[0][lo:hi], ny + extra[1][lo:hi]
        dst[0][lo:hi] = nx
        dst[1][lo:hi] = ny


def line_steps(jobs, co, chunk=16):
    first = min((rows[0] for _, _, rows in jobs), default=0)
    last = max((rows[1] for _, _, rows in jobs), default=0)
    for r in range(first, last, chunk):
        for src, dst, (lo, hi) in jobs:
            part = max(lo, r), min(hi, r + chunk)
            if part[0] < part[1]:
                step(src, dst, part, co, chunk=chunk)


def kernel(
    u_ref, v_ref, cls_ref, act_ref, out_ref,
    uw, vw, ocls, oact, ncls, nact, tab, mask, cf, cg, fx, fy, px, py, dx, dy, lx, ly, ex, ey, rx, ry, send,
    sx, sy, tx, ty, qx, qy, wf, wg, sf, sg, part, rin,
    lsem, ssem, rsem, xs, xr, ps, pr, ready,
):
    t, s = lax.axis_index("tm"), lax.axis_index("space")
    chip, core = lax.div(t, 2), lax.rem(t, 2)
    far = lax.div(lax.rem(s, 4), 2)
    half = (1 - core) * (1 - far) + core * far
    beside = s + 2 * half - 1
    there = lax.div(lax.rem(beside + 4, 4), 2)
    other = half * (1 - there) + (1 - half) * there
    peer = {"tm": 2 * chip + other, "space": lax.rem(beside + 16, 16)}
    has_peer = (beside >= 0) & (beside < 16)
    mate = {"tm": t + 1 - 2 * core}

    barrier = pltpu.get_barrier_semaphore()
    pl.semaphore_signal(barrier, inc=1, device_id=mate, device_id_type=MESH)

    @pl.when(has_peer)
    def _():
        pl.semaphore_signal(barrier, inc=1, device_id=peer, device_id_type=MESH)

    for a, b in ((0, 1), (2, 1), (3, 1), (1, 2), (3, 2)):

        @pl.when(chip == a)
        def _(b=b):
            pl.semaphore_signal(barrier, inc=1, device_id={"tm": 2 * b + core}, device_id_type=MESH)

    here = pl.multiple_of(80 * half, 8)
    into = pl.multiple_of(GHOST * (1 - half), 8)
    local = [
        pltpu.make_async_copy(u_ref.at[pl.ds(here, LOCAL)], uw.at[pl.ds(into, LOCAL)], lsem.at[0]),
        pltpu.make_async_copy(v_ref.at[pl.ds(here, LOCAL)], vw.at[pl.ds(into, LOCAL)], lsem.at[1]),
        pltpu.make_async_copy(cls_ref, ocls, lsem.at[2]),
        pltpu.make_async_copy(act_ref, oact, lsem.at[3]),
    ]
    for c in local:
        c.start()
    for buf in (fx, fy):
        for k in range(2):
            buf[k, :PAD] = jnp.zeros((PAD, W), jnp.float32)
            buf[k, PAD + WIN :] = jnp.zeros((PAD, W), jnp.float32)

    def tables(edges_here):
        wi = lax.broadcasted_iota(jnp.int32, (32, 32), 0) + (16 * half - GHOST // BR)
        lane = lax.broadcasted_iota(jnp.int32, (32, 32), 1)
        own = (wi >= 0) & (wi < 32)
        hot = lane == jnp.where(wi < 0, wi + 32, jnp.where(wi >= 32, wi - 32, wi))
        gi = wi + 32 * s
        inside = (gi >= 0) & (gi < 512)
        cls = jnp.broadcast_to(ocls[...], (32, 32))
        act = jnp.broadcast_to(oact[...], (32, 32))
        if edges_here:
            cls = jnp.where(own, cls, jnp.broadcast_to(ncls[...], (32, 32)))
            act = jnp.where(own, act, jnp.broadcast_to(nact[...], (32, 32)))
        cls = jnp.where(hot, cls.astype(jnp.float32), 0.0)
        act = jnp.where(hot & inside, act.astype(jnp.float32), 0.0)
        cls = jnp.broadcast_to(jnp.sum(cls, axis=1, keepdims=True), (32, W))
        act = jnp.broadcast_to(jnp.sum(act, axis=1, keepdims=True), (32, W))
        gain = pick(cls, row_gains)
        tab[0, 8:40] = gain * act
        tab[1, 8:40] = act
        tab[2, 8:40] = gain
        tab[3, 8:40] = pick(cls, column_gains) * act
        tab[4, 8:40] = pick(cls, rate_gains) * act
        tab[1, 0:8] = jnp.zeros((8, W), jnp.float32)
        tab[2, 0:8] = jnp.zeros((8, W), jnp.float32)
        tab[5, 8:40] = 0.5 * (tab[2, 8:40] + tab[2, 7:39]) * tab[1, 8:40] * tab[1, 7:39]
        lanes = lax.broadcasted_iota(jnp.int32, (8, W), 1)
        sub = lax.broadcasted_iota(jnp.int32, (8, W), 0)
        first, last = lanes == 0, lanes == W - 1
        ends = jnp.where(first | last, 1.0, 2.0)
        for b in range(NBLK):

            def row(q, k):
                return jnp.broadcast_to(tab[q, 8 + k : 9 + k], (8, W))

            bu = jnp.where(sub == 0, row(5, b), row(0, b))
            bd = jnp.where(sub == 7, row(5, b + 1), row(0, b))
            cc, rr = row(3, b), row(4, b)
            for co, h, sc in ((cf, HF, SF), (cg, HG, SG)):
                at = slice(8 * b, 8 * b + 8)
                co[0, at] = (1.0 + h) - h * (bu + bd + cc * ends)
                co[1, at] = h * bu
                co[2, at] = h * bd
                co[3, at] = jnp.where(first, 0.0, h * cc)
                co[4, at] = jnp.where(last, 0.0, h * cc)
                co[5, at] = (h * h) * rr
                co[6, at] = 1.0 - (0.8 * h) * rr
                co[7, at] = (0.7 * h * h / sc) * rr
            if GHOST // BR <= b < (GHOST + HALF) // BR:
                mask[8 * b - GHOST : 8 * b - GHOST + 8] = row(1, b)

    def rescaled(src, dst, rows, ax, ay):
        at = slice(rows[0] + PAD, rows[1] + PAD)
        dst[0][at] = src[0][at] * ax
        dst[1][at] = src[1][at] * ay

    fine = [(fx.at[k], fy.at[k]) for k in range(2)]
    points = [(px.at[k], py.at[k]) for k in range(14)]
    shift = (dx, dy)
    chain = [(rx.at[k], ry.at[k]) for k in range(4)]

    def prepare(span, ghost, last, co, cg):
        for i in range(16):
            step(fine[i % 2], fine[(i + 1) % 2], span(ghost - 1 - i), co)
            if i == 7:
                rescaled(fine[0], points[0], span(ghost - 8), CX, CY)
        rescaled(fine[0], points[1], span(ghost - 16), CX, CY)
        step(points[0], shift, span(ghost - 17), cg)
        lo, hi = (e + PAD for e in span(ghost - 17))
        dx[lo:hi] = px[1, lo:hi] - dx[lo:hi]
        dy[lo:hi] = py[1, lo:hi] - dy[lo:hi]
        go_on(span, ghost, 3, last, cg)

    def go_on(span, ghost, first, last, cg):
        for j in range(first, last + 1):
            step(points[j - 2], points[j - 1], span(ghost - 14 - j), cg, shift)

    def begins(a):
        return pl.multiple_of(SHARE * (a + (2 - 2 * a) * half), 8)

    def sending(a, b):
        return pltpu.make_async_remote_copy(
            src_ref=part.at[b - 1], dst_ref=rin.at[:, pl.ds(begins(a), SHARE)], send_sem=ps.at[b - 1], recv_sem=pr.at[a],
            device_id={"tm": 2 * b + core}, device_id_type=MESH,
        )

    wide = functools.partial(span, side=REACH, rows=SHARE)

    def share_begins():
        base = pl.multiple_of(GHOST - 8 - REACH + begins(chip), 8)
        long = SHARE + 2 * REACH
        inner = pl.multiple_of(base + REACH - SIDE, 8)
        for q in range(8):
            wf[q] = cf[q, pl.ds(base, long)]
            wg[q] = cg[q, pl.ds(base, long)]
            sf[q] = cf[q, pl.ds(inner, SHARE + 2 * SIDE)]
            sg[q] = cg[q, pl.ds(inner, SHARE + 2 * SIDE)]
        fx[0, PAD : PAD + long] = uw[pl.ds(base, long)] * (1.0 / SF)
        fy[0, PAD : PAD + long] = vw[pl.ds(base, long)] * (HF / SF)
        prepare(wide, REACH, 2, wf, wg)

    def share():
        at = slice(PAD + REACH - SIDE, PAD + REACH + SHARE + SIDE)
        own = slice(PAD, PAD + SHARE + 2 * SIDE)
        mid = slice(PAD + SIDE, PAD + SIDE + SHARE)
        rows = functools.partial(span, side=SIDE, rows=SHARE)

        def line(m, i):
            return sx.at[m % 2, i], sy.at[m % 2, i]

        def link(i):
            return tx.at[i], ty.at[i]

        for tick in range(16 + NL):
            if 0 <= tick < NL - 1:
                go_on(wide, REACH, tick + 3, tick + 3, wg)
            if 0 <= tick < NL:
                sx[0, tick, own] = px[tick + 1, at] * (1.0 / CX)
                sy[0, tick, own] = py[tick + 1, at] * (1.0 / CY)
            i = tick - 16
            if 0 <= i < NL:
                if i == 0:
                    rescaled(line(0, 0), link(0), rows(8), CX, CY)
                else:
                    lo, hi = (e + PAD for e in rows(8 - i))
                    qx[i, lo:hi] = sx[0, i, lo:hi] * CX - qx[i, lo:hi]
                    qy[i, lo:hi] = sy[0, i, lo:hi] * CY - qy[i, lo:hi]
                    step(link(i - 1), link(i), rows(8 - i), sg, (qx.at[i], qy.at[i]))
                if i % 4 == 0:
                    b = i // 4
                    part[b, 0] = tx[i, mid]
                    part[b, 1] = ty[i, mid]
            line_steps(
                [
                    (line(m, i), line(m + 1, i), rows(23 - i - m))
                    for i in range(NL)
                    for m in (tick - i,)
                    if 0 <= m < 16
                ],
                sf,
            )
            i = tick - 7
            if 1 <= i < NL:
                rescaled(line(0, i), line(1, i), rows(16 - i), CX, CY)
                step(line(1, i), (qx.at[i], qy.at[i]), rows(8 - i), sg)

            i = tick - 16
            if i in (0, 4, 8):

                @pl.when(chip == 0)
                def _():
                    if i == 0:
                        pl.semaphore_wait(ready, 1)

                b = i // 4 + 1
                for a in range(3):

                    @pl.when(chip == a)
                    def _(a=a, b=b):
                        if a != b:
                            sending(a, b).start()
                        else:
                            rin[:, pl.ds(begins(a), SHARE)] = part[b - 1]

    @pl.when((chip == 1) | (chip == 2))
    def _():
        for c in local:
            c.wait()
        tables(False)
        share_begins()

    pl.semaphore_wait(barrier, 1 + has_peer.astype(jnp.int32) + jnp.where(chip == 1, 3, jnp.where(chip == 2, 2, 0)))
    edge = pl.multiple_of((ROWS - GHOST) * half, 8)
    land = pl.multiple_of(LOCAL * (1 - half), 8)
    mine = pl.multiple_of(LOCAL * half, 8)
    edges = [
        (cls_ref, ncls),
        (act_ref, nact),
        (u_ref.at[pl.ds(edge, GHOST)], uw.at[pl.ds(land, GHOST)]),
        (v_ref.at[pl.ds(edge, GHOST)], vw.at[pl.ds(land, GHOST)]),
    ]
    remote = [
        pltpu.make_async_remote_copy(
            src_ref=a, dst_ref=b, send_sem=ssem.at[i], recv_sem=rsem.at[i], device_id=peer, device_id_type=MESH
        )
        for i, (a, b) in enumerate(edges)
    ]

    @pl.when(has_peer)
    def _():
        for c in remote:
            c.start()

    @pl.when(chip == 1)
    def _():
        pl.semaphore_signal(ready, inc=1, device_id={"tm": core}, device_id_type=MESH)

    @pl.when((chip == 0) | (chip == 3))
    def _():
        for c in local:
            c.wait()

    def edges_in():
        @pl.when(has_peer)
        def _():
            remote[0].wait_recv()
            remote[1].wait_recv()

        @pl.when(jnp.logical_not(has_peer))
        def _():
            ncls[...] = jnp.zeros((1, 32), jnp.int32)
            nact[...] = jnp.zeros((1, 32), jnp.int32)
            uw[pl.ds(mine, GHOST)] = jnp.zeros((GHOST, W), jnp.float32)
            vw[pl.ds(mine, GHOST)] = jnp.zeros((GHOST, W), jnp.float32)

        tables(True)

        @pl.when(has_peer)
        def _():
            remote[2].wait_recv()
            remote[3].wait_recv()

    @pl.when(chip == 0)
    def _():
        edges_in()
        share_begins()

    @pl.when(chip < 3)
    def _():
        share()

    @pl.when(chip > 0)
    def _():
        edges_in()

    fx[0, PAD : PAD + WIN] = uw[...] * (1.0 / SF)
    fy[0, PAD : PAD + WIN] = vw[...] * (HF / SF)

    @pl.when(chip == 0)
    def _():
        for i in range(32):
            step(fine[i % 2], fine[(i + 1) % 2], span(31 - i), cf)
            if i % 8 == 7:
                rescaled(fine[0], chain[i // 8], span(0), CX, CY)

    @pl.when(chip > 0)
    def _():
        prepare(span, OWN, 6, cf, cg)

    @pl.when(chip > 1)
    def _():
        go_on(span, OWN, 7, 10, cg)

    @pl.when(chip == 3)
    def _():
        go_on(span, OWN, 11, 14, cg)

    @pl.when(chip > 0)
    def _():
        lo, hi = (e + PAD for e in span(19))
        for i in range(4):
            k = 4 * chip - 2 + i
            lx[0, i, lo:hi] = px[k, lo:hi] * (1.0 / CX)
            ly[0, i, lo:hi] = py[k, lo:hi] * (1.0 / CY)
        for m in range(16):
            if m == 8:
                for i in range(4):
                    rescaled((lx.at[0, i], ly.at[0, i]), (lx.at[1, i], ly.at[1, i]), span(11 - i), CX, CY)
                    step((lx.at[1, i], ly.at[1, i]), (ex.at[i], ey.at[i]), span(3 - i), cg)
            a, b = m % 2, (m + 1) % 2
            line_steps(
                [((lx.at[a, i], ly.at[a, i]), (lx.at[b, i], ly.at[b, i]), span(18 - i - m)) for i in range(4)], cf
            )
        for i in range(4):
            lo, hi = (e + PAD for e in span(3 - i))
            ex[i, lo:hi] = lx[0, i, lo:hi] * CX - ex[i, lo:hi]
            ey[i, lo:hi] = ly[0, i, lo:hi] * CY - ey[i, lo:hi]
        for a in range(3):

            @pl.when(chip != a)
            def _(a=a):
                sending(a, 1).wait_recv()

        at = slice(PAD + GHOST - 8, PAD + GHOST + HALF + 8)
        rx[3, at] = rin[0]
        ry[3, at] = rin[1]
        for i in range(4):
            step(chain[(i + 3) % 4], chain[i], span(3 - i), cg, (ex.at[i], ey.at[i]))

    live = mask[...] > 0.5
    mid = slice(PAD + GHOST, PAD + GHOST + HALF)
    held = pl.ds(pl.multiple_of(HALF * half, 8), HALF)
    sends = []
    for i in range(2):
        k = 2 - 2 * core + i
        send[i, 0] = jnp.where(live, rx[k, mid] * SG, uw[GHOST : GHOST + HALF])
        send[i, 1] = jnp.where(live, ry[k, mid] * (SG / HG), vw[GHOST : GHOST + HALF])
        c = pltpu.make_async_remote_copy(
            src_ref=send.at[i], dst_ref=out_ref.at[i, :, held], send_sem=xs.at[i], recv_sem=xr.at[i],
            device_id=mate, device_id_type=MESH,
        )
        c.start()
        sends.append(c)
    for i in range(2):
        k = 2 * core + i
        out_ref[i, 0, held] = jnp.where(live, rx[k, mid] * SG, uw[GHOST : GHOST + HALF])
        out_ref[i, 1, held] = jnp.where(live, ry[k, mid] * (SG / HG), vw[GHOST : GHOST + HALF])
    for c in sends:
        c.wait()
    for a, b in SENDS:

        @pl.when(chip == a)
        def _(a=a, b=b):
            sending(a, b).wait_send()

    @pl.when(has_peer)
    def _():
        for c in remote:
            c.wait_send()


def local(initial_voltage, initial_recovery, block_class, block_active):
    f32, i32 = jnp.float32, jnp.int32
    given = (initial_voltage, initial_recovery, block_class.reshape(1, 32), block_active.reshape(1, 32))
    given = [pltpu.with_memory_space_constraint(x, pltpu.HBM) for x in given]
    full = PAD + WIN + PAD
    share = PAD + SHARE + 2 * SIDE + PAD
    return pl.pallas_call(
        kernel,
        out_shape=jax.ShapeDtypeStruct((2, 2, ROWS, W), f32),
        in_specs=[pl.BlockSpec(memory_space=pltpu.HBM)] * 4,
        out_specs=pl.BlockSpec(memory_space=pltpu.VMEM),
        scratch_shapes=[
            pltpu.VMEM((WIN, W), f32),
            pltpu.VMEM((WIN, W), f32),
            *[pltpu.VMEM((1, 32), i32)] * 4,
            pltpu.VMEM((6, 48, W), f32),
            pltpu.VMEM((HALF, W), f32),
            *[pltpu.VMEM((8, WIN, W), f32)] * 2,
            *[pltpu.VMEM((2, full, W), f32)] * 2,
            *[pltpu.VMEM((14, full, W), f32)] * 2,
            *[pltpu.VMEM((full, W), f32)] * 2,
            *[pltpu.VMEM((2, 4, full, W), f32)] * 2,
            *[pltpu.VMEM((4, full, W), f32)] * 4,
            pltpu.VMEM((2, 2, HALF, W), f32),
            *[pltpu.VMEM((2, NL, share, W), f32)] * 2,
            *[pltpu.VMEM((NL, share, W), f32)] * 4,
            *[pltpu.VMEM((8, SHARE + 2 * REACH, W), f32)] * 2,
            *[pltpu.VMEM((8, SHARE + 2 * SIDE, W), f32)] * 2,
            pltpu.VMEM((3, 2, SHARE, W), f32),
            pltpu.VMEM((2, 144, W), f32),
            pltpu.SemaphoreType.DMA((4,)),
            pltpu.SemaphoreType.DMA((4,)),
            pltpu.SemaphoreType.DMA((4,)),
            pltpu.SemaphoreType.DMA((2,)),
            pltpu.SemaphoreType.DMA((2,)),
            pltpu.SemaphoreType.DMA((3,)),
            pltpu.SemaphoreType.DMA((3,)),
            pltpu.SemaphoreType.REGULAR,
        ],
        compiler_params=pltpu.CompilerParams(
            collective_id=0, has_side_effects=True, vmem_limit_bytes=40 * 1024 * 1024
        ),
    )(*given)


def solution(mesh):
    in_specs = (P("space", None), P("space", None), P("space"), P("space"))
    out_specs = P("tm", None, "space", None)
    return jax.shard_map(local, mesh=mesh, in_specs=in_specs, out_specs=out_specs, check_vma=False)
```
